32 devices in a mesh: gx: 8 (over y, x, core), gy: 4 (over z).
Axes of the slice: x: 2, y: 2, z: 4, core: 2. Of those that a mesh axis runs over, the one named last changes fastest.
Arguments:
- saved_fluid: bfloat16 [3, 19, 8, 64, 512], P(None, None, None, 'gx', 'gy'), may hold values from 0.019897461 to 0.099609375
- saved_tracer: bfloat16 [3, 7, 8, 64, 512], P(None, None, None, 'gx', 'gy'), may hold values from 0.049804688 to 0.25
- adjoint_fluid: float32 [19, 8, 64, 512], P(None, None, 'gx', 'gy'), may hold values from -6 to 6
- adjoint_tracer: float32 [7, 8, 64, 512], P(None, None, 'gx', 'gy'), may hold values from -6 to 6
- label: int32 [8, 64, 512], P(None, 'gx', 'gy'), may hold values from 0 to 2
Outputs:
- fluid_sensitivity: float32 [19, 8, 64, 512], P(None, None, 'gx', 'gy')
- tracer_sensitivity: float32 [7, 8, 64, 512], P(None, None, 'gx', 'gy')
The draws below stay inside these ranges and needn't reach their ends.
Inputs may be any that keep to these rules, and one draw needn't show every extreme that they name: `label`: 0 marks a fluid voxel, 1 solid rock, 2 a fluid voxel at an adsorbing site.
All inputs are finite; a program needn't handle non-finite values.
Results may differ from the reference program's by a relative error of at most 0.0003.
Values sent between devices are 32-bit elements; how exact they have to be, the bound alone decides.
A program may use at most 64 MiB of HBM per device.

```python
import jax
import jax.numpy as jnp
import numpy as np
from jax import lax

Z = 8
STEPS = 3
QF = 19
QT = 7
NX = 64
NY = 512


def place_ends(values, rng, low, high):
    extent = values.shape
    spot = [jax.random.randint(jax.random.fold_in(rng, axis), (), 0, extent[axis]) for axis in range(len(extent))]
    values = values.at[tuple(spot)].set(low)
    longest = extent.index(max(extent))
    spot[longest] = (spot[longest] + 1) % extent[longest]
    return values.at[tuple(spot)].set(high)


def level_of(rng, shape, shards, low, top_value):
    gain = 1.0
    for position, shards_of in shards:
        steps = jax.random.uniform(jax.random.fold_in(jax.random.fold_in(rng, 6), position), (shards_of,), jnp.float32, low / len(shards), top_value / len(shards))
        gain = gain * jnp.repeat(jnp.exp(steps), shape[position] // shards_of).reshape((-1,) + (1,) * (len(shape) - 1 - position))
    return gain


def noise(own_key, extent, deviation, most, split=(), kind=jnp.bfloat16):
    loudness = level_of(own_key, extent, split, -0.22, 0.18) if split else 1.0
    drawn = jax.random.normal(own_key, extent, jnp.float32) * deviation * loudness
    return jnp.minimum(jnp.maximum(drawn, -most), most).astype(kind)


def setup_inputs(seed: int = 0) -> dict:
    key_of = jax.random.split(jax.random.key(seed), 6)
    saved_fluid = jnp.clip(0.019897461 + 0.079711914 * jax.random.uniform(key_of[0], (STEPS, QF, Z, NX, NY), jnp.float32) ** level_of(key_of[0], (STEPS, QF, Z, NX, NY), ((3, 8), (4, 4)), -0.2, 0.2), 0.019897461, 0.099609375).astype(jnp.bfloat16)
    saved_tracer = jnp.clip(0.049804688 + 0.20019531 * jax.random.uniform(key_of[1], (STEPS, QT, Z, NX, NY), jnp.float32) ** level_of(key_of[1], (STEPS, QT, Z, NX, NY), ((3, 8), (4, 4)), -0.2, 0.2), 0.049804688, 0.25).astype(jnp.bfloat16)
    adjoint_fluid = noise(key_of[2], (QF, Z, NX, NY), 1.0, 6.0, ((2, 8), (3, 4)), jnp.float32)
    adjoint_tracer = noise(key_of[3], (QT, Z, NX, NY), 1.0, 6.0, ((2, 8), (3, 4)), jnp.float32)
    label = place_ends(jax.random.randint(key_of[4], (Z, NX, NY), 0, 3), jax.random.fold_in(key_of[4], 1), 0, 2).astype(jnp.int32)
    return dict(saved_fluid=saved_fluid, saved_tracer=saved_tracer, adjoint_fluid=adjoint_fluid, adjoint_tracer=adjoint_tracer, label=label)


TRACER_RATE = 1.3
ADSORB = 0.3

def lattice():
    return np.array([[0, 0, 0], [1, 0, 0], [-1, 0, 0], [0, 1, 0], [0, -1, 0], [0, 0, 1], [0, 0, -1], [1, 1, 0], [-1, -1, 0], [1, -1, 0], [-1, 1, 0], [1, 0, 1], [-1, 0, -1], [1, 0, -1], [-1, 0, 1], [0, 1, 1], [0, -1, -1], [0, 1, -1], [0, -1, 1]])

def opposite(count):
    return [0] + [number + 1 if number % 2 == 1 else number - 1 for number in range(1, count)]

def collision_matrix():
    speeds = lattice()
    along_x, along_y, along_z = (speeds[:, 0], speeds[:, 1], speeds[:, 2])
    square = along_x ** 2 + along_y ** 2 + along_z ** 2
    basis = [np.ones(19), square, square ** 2, along_x, square * along_x, along_y, square * along_y, along_z, square * along_z, 3 * along_x ** 2 - square, square * (3 * along_x ** 2 - square), along_y ** 2 - along_z ** 2, square * (along_y ** 2 - along_z ** 2), along_x * along_y, along_y * along_z, along_x * along_z, along_x * (along_y ** 2 - along_z ** 2), along_y * (along_z ** 2 - along_x ** 2), along_z * (along_x ** 2 - along_y ** 2)]
    built = []
    for vector in basis:
        for other in built:
            vector = vector - vector @ other / (other @ other) * other
        built.append(vector)
    moments = np.stack(built)
    inverse = moments.T / np.sum(moments ** 2, axis=1)
    rates = np.array([0, 1.19, 1.4, 0, 1.2, 0, 1.2, 0, 1.2, 1.25, 1.4, 1.25, 1.4, 1.25, 1.25, 1.25, 1.98, 1.98, 1.98])
    return inverse * rates @ moments

def collide(fluid, tracer, label, table):
    speeds = lattice().astype(np.float32)
    extra = (1,) * (fluid.ndim - 1)
    fluid_weights = np.array([1.0 / 3.0] + [1.0 / 18.0] * 6 + [1.0 / 36.0] * 12, np.float32).reshape((19,) + extra)
    tracer_weights = np.array([0.25] + [0.125] * 6, np.float32).reshape((7,) + extra)
    density = lax.optimization_barrier(jnp.sum(fluid, axis=0))
    velocity = jnp.tensordot(jnp.asarray(speeds.T), fluid, axes=1, precision=lax.Precision.HIGHEST) / density
    projection = jnp.tensordot(jnp.asarray(speeds), velocity, axes=1, precision=lax.Precision.HIGHEST)
    speed_square = lax.optimization_barrier(jnp.sum(velocity * velocity, axis=0))
    equilibrium = fluid_weights * density * (1.0 + 3.0 * projection + 4.5 * projection * projection - 1.5 * speed_square)
    relaxed = fluid - jnp.tensordot(table, fluid - equilibrium, axes=1, precision=lax.Precision.HIGHEST)
    solid = label == 1
    fluid_out = jnp.where(solid, jnp.stack([fluid[other] for other in opposite(19)]), relaxed)
    amount = lax.optimization_barrier(jnp.sum(tracer, axis=0))
    tracer_eq = tracer_weights * amount * (1.0 + 4.0 * projection[:7])
    kept = jnp.where(label == 2, 1.0 - ADSORB, 1.0)
    tracer_relaxed = (tracer - TRACER_RATE * (tracer - tracer_eq)) * kept
    tracer_out = jnp.where(solid, jnp.stack([tracer[other] for other in opposite(7)]), tracer_relaxed)
    return (fluid_out, tracer_out)

def pull(field):
    speeds = lattice()
    return jnp.stack([jnp.roll(field[number], (-int(speeds[number, 2]), -int(speeds[number, 0]), -int(speeds[number, 1])), axis=(0, 1, 2)) for number in range(field.shape[0])])

def reference(saved_fluid, saved_tracer, adjoint_fluid, adjoint_tracer, label):
    table = jnp.asarray(collision_matrix(), jnp.float32)

    def plane_adjoint(operands):
        fluid, tracer, plane_label, pulled_fluid, pulled_tracer = operands
        _, pullback = jax.vjp(lambda first, second: collide(first, second, plane_label, table), fluid, tracer)
        return pullback((pulled_fluid, pulled_tracer))
    for step in reversed(range(STEPS)):
        pulled_fluid = pull(adjoint_fluid)
        pulled_tracer = pull(adjoint_tracer)
        operands = (jnp.swapaxes(saved_fluid[step].astype(jnp.float32), 0, 1), jnp.swapaxes(saved_tracer[step].astype(jnp.float32), 0, 1), label, jnp.swapaxes(pulled_fluid, 0, 1), jnp.swapaxes(pulled_tracer, 0, 1))
        new_fluid, new_tracer = lax.map(plane_adjoint, operands)
        adjoint_fluid = jnp.swapaxes(new_fluid, 0, 1)
        adjoint_tracer = jnp.swapaxes(new_tracer, 0, 1)
    return (adjoint_fluid, adjoint_tracer)
```

```python
import functools

import jax
import jax.numpy as jnp
from jax import lax
from jax.experimental import pallas as pl
from jax.experimental.pallas import tpu as pltpu
from jax.sharding import PartitionSpec as P

TRACER_RATE = 1.3
ADSORB = 0.3
FLOW = [
    (0, 0, 0), (1, 0, 0), (-1, 0, 0), (0, 1, 0), (0, -1, 0), (0, 0, 1), (0, 0, -1),
    (1, 1, 0), (-1, -1, 0), (1, -1, 0), (-1, 1, 0), (1, 0, 1), (-1, 0, -1), (1, 0, -1),
    (-1, 0, 1), (0, 1, 1), (0, -1, -1), (0, 1, -1), (0, -1, 1),
]
SPEEDS = FLOW + FLOW[:7]
COUNT = len(SPEEDS)
X_LISTS = [[1, 7, 9, 11, 13, 20], [2, 8, 10, 12, 14, 21]]
Y_LISTS = [[3, 7, 10, 15, 17, 22], [4, 8, 9, 16, 18, 23]]
CORNERS = [7, 8, 9, 10]
MESH = pl.DeviceIdType.MESH
SLOT = 16


def macros(f, h):
    s = [f[2 * k - 1] + f[2 * k] for k in range(1, 10)]
    d = [f[2 * k - 1] - f[2 * k] for k in range(1, 10)]
    rho = f[0] + ((s[0] + s[1]) + (s[2] + s[3])) + ((s[4] + s[5]) + (s[6] + s[7])) + s[8]
    inv = 1.0 / rho
    ux = (d[0] + (d[3] + d[4]) + (d[5] + d[6])) * inv
    uy = (d[1] + (d[3] - d[4]) + (d[7] + d[8])) * inv
    uz = (d[2] + (d[5] - d[6]) + (d[7] - d[8])) * inv
    amount = h[0] + ((h[1] + h[2]) + (h[3] + h[4])) + (h[5] + h[6])
    return ux, uy, uz, amount * inv * (4.0 * TRACER_RATE * 0.125)


def transpose_collision(p, q, ux, uy, uz, cr, label):
    s = [None] + [p[2 * k - 1] + p[2 * k] for k in range(1, 10)]
    d = [None] + [p[2 * k - 1] - p[2 * k] for k in range(1, 10)]
    kept = jnp.where(label == 2, 1.0 - ADSORB, 1.0)
    tx, ty, tz = q[1] - q[2], q[3] - q[4], q[5] - q[6]
    crk = cr * kept
    bx, by, bz = crk * tx, crk * ty, crk * tz
    total = ((q[1] + q[2]) + (q[3] + q[4])) + (q[5] + q[6])
    drift = ux * tx + uy * ty + uz * tz
    common = (kept * TRACER_RATE) * (0.25 * q[0] + 0.125 * total + 0.5 * drift)
    direct = kept * (1.0 - TRACER_RATE)
    h_out = [direct * value + common for value in q]
    sxy, dxy = s[4] + s[5], s[4] - s[5]
    sxz, dxz = s[6] + s[7], s[6] - s[7]
    syz, dyz = s[8] + s[9], s[8] - s[9]
    axis_sum = (s[1] + s[2]) + s[3]
    edge_sum = (sxy + sxz) + syz
    ce, cs = 1.19 / 2394.0, 1.4 / 252.0
    te = (8.0 * ce) * edge_sum - (11.0 * ce) * axis_sum - (30.0 * ce) * p[0]
    ts = cs * edge_sum - (4.0 * cs) * axis_sum + (12.0 * cs) * p[0]
    rx, ry, rz = s[1] - syz, s[2] - sxz, s[3] - sxy
    r_third = (axis_sum - edge_sum) * (1.0 / 3.0)
    gx, gy, gz = 2.0 * s[1] + syz, 2.0 * s[2] + sxz, 2.0 * s[3] + sxy
    g_third = (2.0 * axis_sum + edge_sum) * (1.0 / 3.0)
    cp, cq = 1.25 * 6.0 / 36.0, 1.4 * 6.0 / 72.0
    px, py, pz = cp * (rx - r_third), cp * (ry - r_third), cp * (rz - r_third)
    wx, wy, wz = cq * (gx - g_third), cq * (gy - g_third), cq * (gz - g_third)
    txy, txz, tyz = (1.25 / 4.0) * dxy, (1.25 / 4.0) * dxz, (1.25 / 4.0) * dyz
    base = 38.0 * te - 11.0 * ts
    sx = base + 2.0 * px + wx
    sy = base + 2.0 * py + wy
    sz = base + 2.0 * pz + wz
    vx = sx * ux + txy * uy + txz * uz
    vy = txy * ux + sy * uy + tyz * uz
    vz = txz * ux + tyz * uy + sz * uz
    nx, ny, nz = vx + bx, vy + by, vz + bz
    shift = ux * (nx - 0.5 * vx) + uy * (ny - 0.5 * vy) + uz * (nz - 0.5 * vz)
    e0 = 9.0 * ts - 19.0 * te + shift
    ea = shift - 7.0 * ts
    ee = 19.0 * te - 2.0 * ts + shift
    even_axis = [ea + px + 2.0 * wx, ea + py + 2.0 * wy, ea + pz + 2.0 * wz]
    exy, exz, eyz = ee - pz + wz, ee - py + wy, ee - px + wx
    axy, bxy = d[4] + d[5], d[4] - d[5]
    axz, bxz = d[6] + d[7], d[6] - d[7]
    ayz, byz = d[8] + d[9], d[8] - d[9]
    ck, cm = 1.2 / 40.0, 1.98 / 8.0
    kx = ck * ((axy + axz) - 4.0 * d[1])
    ky = ck * ((bxy + ayz) - 4.0 * d[2])
    kz = ck * ((bxz + byz) - 4.0 * d[3])
    mx, my, mz = cm * (axy - axz), cm * (ayz - bxy), cm * (bxz - byz)
    jx, jy, jz = (5.0 / 3.0) * kx - nx, (5.0 / 3.0) * ky - ny, (5.0 / 3.0) * kz - nz
    odd_axis = [jx - 5.0 * kx, jy - 5.0 * ky, jz - 5.0 * kz]
    xp, xm, yp, ym, zp, zm = jx + mx, jx - mx, jy + my, jy - my, jz + mz, jz - mz
    even = even_axis + [exy + txy, exy - txy, exz + txz, exz - txz, eyz + tyz, eyz - tyz]
    odd = odd_axis + [xp + ym, xp - ym, xm + zp, xm - zp, yp + zm, yp - zm]
    solid = label == 1
    f_out = [jnp.where(solid, p[0], p[0] - e0)]
    for k in range(9):
        up, down = p[2 * k + 1], p[2 * k + 2]
        f_out.append(jnp.where(solid, down, up - (even[k] + odd[k])))
        f_out.append(jnp.where(solid, up, down - (even[k] - odd[k])))
    h_final = [jnp.where(solid, q[0], h_out[0])]
    for k in range(3):
        h_final.append(jnp.where(solid, q[2 * k + 2], h_out[2 * k + 1]))
        h_final.append(jnp.where(solid, q[2 * k + 1], h_out[2 * k + 2]))
    return f_out, h_final


def kernel(
    sf_hbm, st_hbm, af_hbm, at_hbm, lab_hbm, of_hbm, ot_hbm,
    sf, st, lab, field, macro, send_x, recv_x, send_y, recv_y, recv_c,
    in_sem, out_sem, send_sem, recv_sem,
):
    nx, ny = lax.axis_size("gx"), lax.axis_size("gy")
    mx, my = lax.axis_index("gx"), lax.axis_index("gy")
    steps, planes = sf.shape[0], sf.shape[2]
    rows, lanes = sf.shape[3], sf.shape[4]
    flow = sf.shape[1]
    x_next, x_prior = lax.rem(mx + 1, nx), lax.rem(mx + nx - 1, nx)
    y_next, y_prior = lax.rem(my + 1, ny), lax.rem(my + ny - 1, ny)
    neighbours = [
        (x_prior, my), (x_next, my), (mx, y_prior), (mx, y_next),
        (x_prior, y_prior), (x_next, y_next), (x_prior, y_next), (x_next, y_prior),
    ]
    barrier = pltpu.get_barrier_semaphore()
    for device in neighbours:
        pl.semaphore_signal(barrier, inc=1, device_id=device, device_id_type=MESH)

    loads = [
        pltpu.make_async_copy(af_hbm, field.at[0, pl.ds(0, flow)], in_sem.at[0]),
        pltpu.make_async_copy(at_hbm, field.at[0, pl.ds(flow, COUNT - flow)], in_sem.at[1]),
        pltpu.make_async_copy(sf_hbm, sf, in_sem.at[2]),
        pltpu.make_async_copy(st_hbm, st, in_sem.at[3]),
        pltpu.make_async_copy(lab_hbm, lab, in_sem.at[4]),
    ]
    for load in loads:
        load.start()

    lane = lax.broadcasted_iota(jnp.int32, (rows, lanes), 1)
    row = lax.broadcasted_iota(jnp.int32, (rows, lanes), 0)
    ends = [lane == 0, lane == lanes - 1]
    edges = [row == rows - 1, row == 0]

    def insert(packed, values):
        done = []
        for side in range(2):
            acc = pltpu.roll(packed[side], lanes - SLOT, 1)
            for k, number in enumerate(Y_LISTS[side]):
                target = lanes - SLOT + k
                moved = pltpu.roll(values[number], target + side, 1)
                acc = jnp.where(lane == target, moved, acc)
            done.append(acc)
        return tuple(done)

    def send(step, source):
        for side in range(2):
            at = 0 if side == 0 else rows - 1
            for k, number in enumerate(X_LISTS[side]):
                send_x[step, side, k] = field[source, number, :, at, :]
        pairs = [
            (send_x.at[step, 0], recv_x.at[step, 0]),
            (send_x.at[step, 1], recv_x.at[step, 1]),
            (send_y.at[step, 0], recv_y.at[step, 0]),
            (send_y.at[step, 1], recv_y.at[step, 1]),
            (send_x.at[step, 0, 1], recv_c.at[step, 0]),
            (send_x.at[step, 1, 1], recv_c.at[step, 1]),
            (send_x.at[step, 0, 2], recv_c.at[step, 2]),
            (send_x.at[step, 1, 2], recv_c.at[step, 3]),
        ]
        copies = []
        for number, ((source_ref, target_ref), device) in enumerate(zip(pairs, neighbours)):
            copies.append(
                pltpu.make_async_remote_copy(
                    src_ref=source_ref,
                    dst_ref=target_ref,
                    send_sem=send_sem.at[step, number],
                    recv_sem=recv_sem.at[step, number],
                    device_id=device,
                    device_id_type=MESH,
                )
            )
        for copy in copies:
            copy.start()
        return copies

    loads[0].wait()
    loads[1].wait()

    def first_pack(z, packed):
        values = {n: field[0, n, z] for side in Y_LISTS for n in side}
        return insert(packed, values)

    empty = (jnp.zeros((rows, lanes), jnp.float32),) * 2
    packed = lax.fori_loop(0, planes, first_pack, empty)
    send_y[0, 0] = packed[0]
    send_y[0, 1] = packed[1]
    pl.semaphore_wait(barrier, len(neighbours))
    started = [send(0, 0)]
    for load in loads[2:]:
        load.wait()

    def prepare(index, carry):
        step, z = index // planes, index % planes
        f = [sf[step, n, z].astype(jnp.float32) for n in range(flow)]
        h = [st[step, n, z].astype(jnp.float32) for n in range(COUNT - flow)]
        for k, value in enumerate(macros(f, h)):
            macro[step, k, z] = value
        return carry

    lax.fori_loop(0, steps * planes, prepare, 0)

    stores = []
    for step in range(steps):
        saved = steps - 1 - step
        source, target = step % 2, (step + 1) % 2
        for copy in started[step]:
            copy.wait_recv()
        for corner, number in enumerate(CORNERS):
            side = 0 if SPEEDS[number][0] == 1 else 1
            end = ends[0] if SPEEDS[number][1] == 1 else ends[1]
            k = X_LISTS[side].index(number)
            recv_x[step, side, k] = jnp.where(end, recv_c[step, corner], recv_x[step, side, k])
        last = step == steps - 1

        def plane(z, carry):
            got, packed = carry
            pulled = []
            for number in range(COUNT):
                cx, cy, cz = SPEEDS[number]
                zz = lax.rem(z + (cz + planes), planes) if cz else z
                value = field[source, number, zz]
                if cy:
                    side = 0 if cy == 1 else 1
                    at = (SLOT * cz) % lanes + Y_LISTS[side].index(number)
                    to = 0 if cy == 1 else lanes - 1
                    column = pltpu.roll(got[side], (to - at) % lanes, 1)
                    value = jnp.where(ends[side], column, value)
                if cx:
                    side = 0 if cx == 1 else 1
                    k = X_LISTS[side].index(number)
                    value = pltpu.roll(value, rows - 1 if cx == 1 else 1, 0)
                    halo = jnp.broadcast_to(recv_x[step, side, k, pl.ds(zz, 1), :], (rows, lanes))
                    value = jnp.where(edges[side], halo, value)
                if cy:
                    value = pltpu.roll(value, lanes - 1 if cy == 1 else 1, 1)
                pulled.append(value)
            ux, uy, uz, cr = [macro[saved, k, z] for k in range(4)]
            f_out, h_out = transpose_collision(
                pulled[:flow], pulled[flow:], ux, uy, uz, cr, lab[z]
            )
            values = f_out + h_out
            for number in range(COUNT):
                field[target, number, z] = values[number]
            if last:
                return got, packed
            got = tuple(pltpu.roll(value, lanes - SLOT, 1) for value in got)
            return got, insert(packed, values)

        def last_plane(z, carry):
            carry = plane(z, carry)
            got, packed = carry
            got = tuple(pltpu.roll(value, lanes - SLOT, 1) for value in got)
            return got, packed

        got = (recv_y[step, 0], recv_y[step, 1])
        got, packed = lax.fori_loop(0, planes, last_plane if last else plane, (got, empty))
        if not last:
            send_y[step + 1, 0] = packed[0]
            send_y[step + 1, 1] = packed[1]
            started.append(send(step + 1, target))
    final = steps % 2
    stores = [
        pltpu.make_async_copy(field.at[final, pl.ds(0, flow)], of_hbm, out_sem.at[0]),
        pltpu.make_async_copy(field.at[final, pl.ds(flow, COUNT - flow)], ot_hbm, out_sem.at[1]),
    ]
    for store in stores:
        store.start()
    for copies in started:
        for copy in copies:
            copy.wait_send()
    for store in stores:
        store.wait()


def body(saved_fluid, saved_tracer, adjoint_fluid, adjoint_tracer, label):
    steps, flow, planes, rows, lanes = saved_fluid.shape
    tracer = saved_tracer.shape[1]
    f32 = jnp.float32
    tile = (rows, lanes)
    return pl.pallas_call(
        kernel,
        out_shape=(
            jax.ShapeDtypeStruct(adjoint_fluid.shape, f32),
            jax.ShapeDtypeStruct(adjoint_tracer.shape, f32),
        ),
        in_specs=[pl.BlockSpec(memory_space=pl.ANY)] * 5,
        out_specs=[pl.BlockSpec(memory_space=pl.ANY)] * 2,
        scratch_shapes=[
            pltpu.VMEM(saved_fluid.shape, saved_fluid.dtype),
            pltpu.VMEM(saved_tracer.shape, saved_tracer.dtype),
            pltpu.VMEM(label.shape, label.dtype),
            pltpu.VMEM((2, flow + tracer, planes) + tile, f32),
            pltpu.VMEM((steps, 4, planes) + tile, f32),
            pltpu.VMEM((steps, 2, 6, planes, lanes), f32),
            pltpu.VMEM((steps, 2, 6, planes, lanes), f32),
            pltpu.VMEM((steps, 2) + tile, f32),
            pltpu.VMEM((steps, 2) + tile, f32),
            pltpu.VMEM((steps, 4, planes, lanes), f32),
            pltpu.SemaphoreType.DMA((5,)),
            pltpu.SemaphoreType.DMA((2,)),
            pltpu.SemaphoreType.DMA((steps, 8)),
            pltpu.SemaphoreType.DMA((steps, 8)),
        ],
        compiler_params=pltpu.CompilerParams(
            collective_id=0, has_side_effects=True, vmem_limit_bytes=32 * 1024 * 1024
        ),
        name="adjoint_steps",
    )(saved_fluid, saved_tracer, adjoint_fluid, adjoint_tracer, label)


def solution(mesh):
    placed = (
        P(None, None, None, "gx", "gy"),
        P(None, None, None, "gx", "gy"),
        P(None, None, "gx", "gy"),
        P(None, None, "gx", "gy"),
        P(None, "gx", "gy"),
    )
    return jax.shard_map(
        body,
        mesh=mesh,
        in_specs=placed,
        out_specs=(P(None, None, "gx", "gy"), P(None, None, "gx", "gy")),
        check_vma=False,
    )
```

```python
import functools

import jax
import jax.numpy as jnp
from jax import lax
from jax.experimental import pallas as pl
from jax.experimental.pallas import tpu as pltpu
from jax.sharding import PartitionSpec as P

TRACER_RATE = 1.3
ADSORB = 0.3
FLOW = [
    (0, 0, 0), (1, 0, 0), (-1, 0, 0), (0, 1, 0), (0, -1, 0), (0, 0, 1), (0, 0, -1),
    (1, 1, 0), (-1, -1, 0), (1, -1, 0), (-1, 1, 0), (1, 0, 1), (-1, 0, -1), (1, 0, -1),
    (-1, 0, 1), (0, 1, 1), (0, -1, -1), (0, 1, -1), (0, -1, 1),
]
SPEEDS = FLOW + FLOW[:7]
COUNT = len(SPEEDS)
X_LISTS = [[1, 7, 9, 11, 13, 20], [2, 8, 10, 12, 14, 21]]
Y_LISTS = [[3, 7, 10, 15, 17, 22], [4, 8, 9, 16, 18, 23]]
CORNERS = [7, 8, 9, 10]
MESH = pl.DeviceIdType.MESH
SLOT = 16


def macros(f, h):
    s = [f[2 * k - 1] + f[2 * k] for k in range(1, 10)]
    d = [f[2 * k - 1] - f[2 * k] for k in range(1, 10)]
    rho = f[0] + ((s[0] + s[1]) + (s[2] + s[3])) + ((s[4] + s[5]) + (s[6] + s[7])) + s[8]
    inv = 1.0 / rho
    ux = (d[0] + (d[3] + d[4]) + (d[5] + d[6])) * inv
    uy = (d[1] + (d[3] - d[4]) + (d[7] + d[8])) * inv
    uz = (d[2] + (d[5] - d[6]) + (d[7] - d[8])) * inv
    amount = h[0] + ((h[1] + h[2]) + (h[3] + h[4])) + (h[5] + h[6])
    return ux, uy, uz, amount * inv * (4.0 * TRACER_RATE * 0.125)


def transpose_collision(p, q, ux, uy, uz, cr, label):
    s = [None] + [p[2 * k - 1] + p[2 * k] for k in range(1, 10)]
    d = [None] + [p[2 * k - 1] - p[2 * k] for k in range(1, 10)]
    kept = jnp.where(label == 2, 1.0 - ADSORB, 1.0)
    tx, ty, tz = q[1] - q[2], q[3] - q[4], q[5] - q[6]
    crk = cr * kept
    bx, by, bz = crk * tx, crk * ty, crk * tz
    total = ((q[1] + q[2]) + (q[3] + q[4])) + (q[5] + q[6])
    drift = ux * tx + uy * ty + uz * tz
    common = (kept * TRACER_RATE) * (0.25 * q[0] + 0.125 * total + 0.5 * drift)
    direct = kept * (1.0 - TRACER_RATE)
    h_out = [direct * value + common for value in q]
    sxy, dxy = s[4] + s[5], s[4] - s[5]
    sxz, dxz = s[6] + s[7], s[6] - s[7]
    syz, dyz = s[8] + s[9], s[8] - s[9]
    axis_sum = (s[1] + s[2]) + s[3]
    edge_sum = (sxy + sxz) + syz
    ce, cs = 1.19 / 2394.0, 1.4 / 252.0
    te = (8.0 * ce) * edge_sum - (11.0 * ce) * axis_sum - (30.0 * ce) * p[0]
    ts = cs * edge_sum - (4.0 * cs) * axis_sum + (12.0 * cs) * p[0]
    rx, ry, rz = s[1] - syz, s[2] - sxz, s[3] - sxy
    r_third = (axis_sum - edge_sum) * (1.0 / 3.0)
    gx, gy, gz = 2.0 * s[1] + syz, 2.0 * s[2] + sxz, 2.0 * s[3] + sxy
    g_third = (2.0 * axis_sum + edge_sum) * (1.0 / 3.0)
    cp, cq = 1.25 * 6.0 / 36.0, 1.4 * 6.0 / 72.0
    px, py, pz = cp * (rx - r_third), cp * (ry - r_third), cp * (rz - r_third)
    wx, wy, wz = cq * (gx - g_third), cq * (gy - g_third), cq * (gz - g_third)
    txy, txz, tyz = (1.25 / 4.0) * dxy, (1.25 / 4.0) * dxz, (1.25 / 4.0) * dyz
    base = 38.0 * te - 11.0 * ts
    sx = base + 2.0 * px + wx
    sy = base + 2.0 * py + wy
    sz = base + 2.0 * pz + wz
    vx = sx * ux + txy * uy + txz * uz
    vy = txy * ux + sy * uy + tyz * uz
    vz = txz * ux + tyz * uy + sz * uz
    nx, ny, nz = vx + bx, vy + by, vz + bz
    shift = ux * (nx - 0.5 * vx) + uy * (ny - 0.5 * vy) + uz * (nz - 0.5 * vz)
    e0 = 9.0 * ts - 19.0 * te + shift
    ea = shift - 7.0 * ts
    ee = 19.0 * te - 2.0 * ts + shift
    even_axis = [ea + px + 2.0 * wx, ea + py + 2.0 * wy, ea + pz + 2.0 * wz]
    exy, exz, eyz = ee - pz + wz, ee - py + wy, ee - px + wx
    axy, bxy = d[4] + d[5], d[4] - d[5]
    axz, bxz = d[6] + d[7], d[6] - d[7]
    ayz, byz = d[8] + d[9], d[8] - d[9]
    ck, cm = 1.2 / 40.0, 1.98 / 8.0
    kx = ck * ((axy + axz) - 4.0 * d[1])
    ky = ck * ((bxy + ayz) - 4.0 * d[2])
    kz = ck * ((bxz + byz) - 4.0 * d[3])
    mx, my, mz = cm * (axy - axz), cm * (ayz - bxy), cm * (bxz - byz)
    jx, jy, jz = (5.0 / 3.0) * kx - nx, (5.0 / 3.0) * ky - ny, (5.0 / 3.0) * kz - nz
    odd_axis = [jx - 5.0 * kx, jy - 5.0 * ky, jz - 5.0 * kz]
    xp, xm, yp, ym, zp, zm = jx + mx, jx - mx, jy + my, jy - my, jz + mz, jz - mz
    even = even_axis + [exy + txy, exy - txy, exz + txz, exz - txz, eyz + tyz, eyz - tyz]
    odd = odd_axis + [xp + ym, xp - ym, xm + zp, xm - zp, yp + zm, yp - zm]
    solid = label == 1
    f_out = [jnp.where(solid, p[0], p[0] - e0)]
    for k in range(9):
        up, down = p[2 * k + 1], p[2 * k + 2]
        f_out.append(jnp.where(solid, down, up - (even[k] + odd[k])))
        f_out.append(jnp.where(solid, up, down - (even[k] - odd[k])))
    h_final = [jnp.where(solid, q[0], h_out[0])]
    for k in range(3):
        h_final.append(jnp.where(solid, q[2 * k + 2], h_out[2 * k + 1]))
        h_final.append(jnp.where(solid, q[2 * k + 1], h_out[2 * k + 2]))
    return f_out, h_final


def kernel(
    sf_hbm, st_hbm, af_hbm, at_hbm, lab_hbm, of_hbm, ot_hbm,
    sf, st, lab, field, macro, send_x, recv_x, send_y, recv_y, recv_c,
    in_sem, out_sem, send_sem, recv_sem,
):
    nx, ny = lax.axis_size("gx"), lax.axis_size("gy")
    mx, my = lax.axis_index("gx"), lax.axis_index("gy")
    steps, planes = sf.shape[0], sf.shape[2]
    rows, lanes = sf.shape[3], sf.shape[4]
    flow = sf.shape[1]
    x_next, x_prior = lax.rem(mx + 1, nx), lax.rem(mx + nx - 1, nx)
    y_next, y_prior = lax.rem(my + 1, ny), lax.rem(my + ny - 1, ny)
    neighbours = [
        (x_prior, my), (x_next, my), (mx, y_prior), (mx, y_next),
        (x_prior, y_prior), (x_next, y_next), (x_prior, y_next), (x_next, y_prior),
    ]
    barrier = pltpu.get_barrier_semaphore()
    for device in neighbours:
        pl.semaphore_signal(barrier, inc=1, device_id=device, device_id_type=MESH)

    loads = [
        pltpu.make_async_copy(af_hbm, field.at[0, pl.ds(0, flow)], in_sem.at[0]),
        pltpu.make_async_copy(at_hbm, field.at[0, pl.ds(flow, COUNT - flow)], in_sem.at[1]),
        pltpu.make_async_copy(sf_hbm, sf, in_sem.at[2]),
        pltpu.make_async_copy(st_hbm, st, in_sem.at[3]),
        pltpu.make_async_copy(lab_hbm, lab, in_sem.at[4]),
    ]
    for load in loads:
        load.start()

    lane = lax.broadcasted_iota(jnp.int32, (rows, lanes), 1)
    row = lax.broadcasted_iota(jnp.int32, (rows, lanes), 0)
    ends = [lane == 0, lane == lanes - 1]
    edges = [row == rows - 1, row == 0]

    def insert(packed, values):
        done = []
        for side in range(2):
            acc = pltpu.roll(packed[side], lanes - SLOT, 1)
            for k, number in enumerate(Y_LISTS[side]):
                target = lanes - SLOT + k
                moved = pltpu.roll(values[number], target + side, 1)
                acc = jnp.where(lane == target, moved, acc)
            done.append(acc)
        return tuple(done)

    def send(step, source):
        for side in range(2):
            at = 0 if side == 0 else rows - 1
            for k, number in enumerate(X_LISTS[side]):
                send_x[step, side, k] = field[source, number, :, at, :]
        pairs = [
            (send_x.at[step, 0], recv_x.at[step, 0]),
            (send_x.at[step, 1], recv_x.at[step, 1]),
            (send_y.at[step, 0], recv_y.at[step, 0]),
            (send_y.at[step, 1], recv_y.at[step, 1]),
            (send_x.at[step, 0, 1], recv_c.at[step, 0]),
            (send_x.at[step, 1, 1], recv_c.at[step, 1]),
            (send_x.at[step, 0, 2], recv_c.at[step, 2]),
            (send_x.at[step, 1, 2], recv_c.at[step, 3]),
        ]
        copies = []
        for number, ((source_ref, target_ref), device) in enumerate(zip(pairs, neighbours)):
            copies.append(
                pltpu.make_async_remote_copy(
                    src_ref=source_ref,
                    dst_ref=target_ref,
                    send_sem=send_sem.at[step, number],
                    recv_sem=recv_sem.at[step, number],
                    device_id=device,
                    device_id_type=MESH,
                )
            )
        for copy in copies:
            copy.start()
        return copies

    loads[0].wait()
    loads[1].wait()

    def first_pack(z, packed):
        values = {n: field[0, n, z] for side in Y_LISTS for n in side}
        return insert(packed, values)

    empty = (jnp.zeros((rows, lanes), jnp.float32),) * 2
    packed = lax.fori_loop(0, planes, first_pack, empty, unroll=8)
    send_y[0, 0] = packed[0]
    send_y[0, 1] = packed[1]
    pl.semaphore_wait(barrier, len(neighbours))
    started = [send(0, 0)]
    for load in loads[2:]:
        load.wait()

    def prepare(index, carry):
        step, z = index // planes, index % planes
        f = [sf[step, n, z].astype(jnp.float32) for n in range(flow)]
        h = [st[step, n, z].astype(jnp.float32) for n in range(COUNT - flow)]
        for k, value in enumerate(macros(f, h)):
            macro[step, k, z] = value
        return carry

    lax.fori_loop(0, steps * planes, prepare, 0, unroll=4)

    stores = []
    for step in range(steps):
        saved = steps - 1 - step
        source, target = step % 2, (step + 1) % 2
        for copy in started[step]:
            copy.wait_recv()
        for corner, number in enumerate(CORNERS):
            side = 0 if SPEEDS[number][0] == 1 else 1
            end = ends[0] if SPEEDS[number][1] == 1 else ends[1]
            k = X_LISTS[side].index(number)
            recv_x[step, side, k] = jnp.where(end, recv_c[step, corner], recv_x[step, side, k])
        last = step == steps - 1

        def plane(z, carry):
            got, packed = carry
            pulled = []
            for number in range(COUNT):
                cx, cy, cz = SPEEDS[number]
                zz = lax.rem(z + (cz + planes), planes) if cz else z
                value = field[source, number, zz]
                if cy:
                    side = 0 if cy == 1 else 1
                    at = (SLOT * cz) % lanes + Y_LISTS[side].index(number)
                    to = 0 if cy == 1 else lanes - 1
                    column = pltpu.roll(got[side], (to - at) % lanes, 1)
                    value = jnp.where(ends[side], column, value)
                if cx:
                    side = 0 if cx == 1 else 1
                    k = X_LISTS[side].index(number)
                    value = pltpu.roll(value, rows - 1 if cx == 1 else 1, 0)
                    halo = jnp.broadcast_to(recv_x[step, side, k, pl.ds(zz, 1), :], (rows, lanes))
                    value = jnp.where(edges[side], halo, value)
                if cy:
                    value = pltpu.roll(value, lanes - 1 if cy == 1 else 1, 1)
                pulled.append(value)
            ux, uy, uz, cr = [macro[saved, k, z] for k in range(4)]
            f_out, h_out = transpose_collision(
                pulled[:flow], pulled[flow:], ux, uy, uz, cr, lab[z]
            )
            values = f_out + h_out
            for number in range(COUNT):
                field[target, number, z] = values[number]
            if last:
                return got, packed
            got = tuple(pltpu.roll(value, lanes - SLOT, 1) for value in got)
            return got, insert(packed, values)

        def last_plane(z, carry):
            carry = plane(z, carry)
            got, packed = carry
            got = tuple(pltpu.roll(value, lanes - SLOT, 1) for value in got)
            return got, packed

        got = (recv_y[step, 0], recv_y[step, 1])
        got, packed = lax.fori_loop(0, planes, last_plane if last else plane, (got, empty), unroll=8)
        if not last:
            send_y[step + 1, 0] = packed[0]
            send_y[step + 1, 1] = packed[1]
            started.append(send(step + 1, target))
    final = steps % 2
    stores = [
        pltpu.make_async_copy(field.at[final, pl.ds(0, flow)], of_hbm, out_sem.at[0]),
        pltpu.make_async_copy(field.at[final, pl.ds(flow, COUNT - flow)], ot_hbm, out_sem.at[1]),
    ]
    for store in stores:
        store.start()
    for copies in started:
        for copy in copies:
            copy.wait_send()
    for store in stores:
        store.wait()


def body(saved_fluid, saved_tracer, adjoint_fluid, adjoint_tracer, label):
    steps, flow, planes, rows, lanes = saved_fluid.shape
    tracer = saved_tracer.shape[1]
    f32 = jnp.float32
    tile = (rows, lanes)
    return pl.pallas_call(
        kernel,
        out_shape=(
            jax.ShapeDtypeStruct(adjoint_fluid.shape, f32),
            jax.ShapeDtypeStruct(adjoint_tracer.shape, f32),
        ),
        in_specs=[pl.BlockSpec(memory_space=pl.ANY)] * 5,
        out_specs=[pl.BlockSpec(memory_space=pl.ANY)] * 2,
        scratch_shapes=[
            pltpu.VMEM(saved_fluid.shape, saved_fluid.dtype),
            pltpu.VMEM(saved_tracer.shape, saved_tracer.dtype),
            pltpu.VMEM(label.shape, label.dtype),
            pltpu.VMEM((2, flow + tracer, planes) + tile, f32),
            pltpu.VMEM((steps, 4, planes) + tile, f32),
            pltpu.VMEM((steps, 2, 6, planes, lanes), f32),
            pltpu.VMEM((steps, 2, 6, planes, lanes), f32),
            pltpu.VMEM((steps, 2) + tile, f32),
            pltpu.VMEM((steps, 2) + tile, f32),
            pltpu.VMEM((steps, 4, planes, lanes), f32),
            pltpu.SemaphoreType.DMA((5,)),
            pltpu.SemaphoreType.DMA((2,)),
            pltpu.SemaphoreType.DMA((steps, 8)),
            pltpu.SemaphoreType.DMA((steps, 8)),
        ],
        compiler_params=pltpu.CompilerParams(
            collective_id=0, has_side_effects=True, vmem_limit_bytes=60 * 1024 * 1024
        ),
        name="adjoint_steps",
    )(saved_fluid, saved_tracer, adjoint_fluid, adjoint_tracer, label)


def solution(mesh):
    placed = (
        P(None, None, None, "gx", "gy"),
        P(None, None, None, "gx", "gy"),
        P(None, None, "gx", "gy"),
        P(None, None, "gx", "gy"),
        P(None, "gx", "gy"),
    )
    return jax.shard_map(
        body,
        mesh=mesh,
        in_specs=placed,
        out_specs=(P(None, None, "gx", "gy"), P(None, None, "gx", "gy")),
        check_vma=False,
    )
```

```python
import functools

import jax
import jax.numpy as jnp
from jax import lax
from jax.experimental import pallas as pl
from jax.experimental.pallas import tpu as pltpu
from jax.sharding import PartitionSpec as P

TRACER_RATE = 1.3
ADSORB = 0.3
FLOW = [
    (0, 0, 0), (1, 0, 0), (-1, 0, 0), (0, 1, 0), (0, -1, 0), (0, 0, 1), (0, 0, -1),
    (1, 1, 0), (-1, -1, 0), (1, -1, 0), (-1, 1, 0), (1, 0, 1), (-1, 0, -1), (1, 0, -1),
    (-1, 0, 1), (0, 1, 1), (0, -1, -1), (0, 1, -1), (0, -1, 1),
]
SPEEDS = FLOW + FLOW[:7]
COUNT = len(SPEEDS)
X_LISTS = [[1, 7, 9, 11, 13, 20], [2, 8, 10, 12, 14, 21]]
Y_LISTS = [[3, 7, 10, 15, 17, 22], [4, 8, 9, 16, 18, 23]]
CORNERS = [7, 8, 9, 10]
MESH = pl.DeviceIdType.MESH
SLOT = 16
IN_SPACE = pltpu.HBM
FIRST_VMEM = 32 * 1024 * 1024


def macros(f, h):
    s = [f[2 * k - 1] + f[2 * k] for k in range(1, 10)]
    d = [f[2 * k - 1] - f[2 * k] for k in range(1, 10)]
    rho = f[0] + ((s[0] + s[1]) + (s[2] + s[3])) + ((s[4] + s[5]) + (s[6] + s[7])) + s[8]
    inv = 1.0 / rho
    ux = (d[0] + (d[3] + d[4]) + (d[5] + d[6])) * inv
    uy = (d[1] + (d[3] - d[4]) + (d[7] + d[8])) * inv
    uz = (d[2] + (d[5] - d[6]) + (d[7] - d[8])) * inv
    amount = h[0] + ((h[1] + h[2]) + (h[3] + h[4])) + (h[5] + h[6])
    return ux, uy, uz, amount * inv * (4.0 * TRACER_RATE * 0.125)


def transpose_collision(p, q, ux, uy, uz, cr, label):
    s = [None] + [p[2 * k - 1] + p[2 * k] for k in range(1, 10)]
    d = [None] + [p[2 * k - 1] - p[2 * k] for k in range(1, 10)]
    kept = jnp.where(label == 2, 1.0 - ADSORB, 1.0)
    tx, ty, tz = q[1] - q[2], q[3] - q[4], q[5] - q[6]
    crk = cr * kept
    bx, by, bz = crk * tx, crk * ty, crk * tz
    total = ((q[1] + q[2]) + (q[3] + q[4])) + (q[5] + q[6])
    drift = ux * tx + uy * ty + uz * tz
    common = (kept * TRACER_RATE) * (0.25 * q[0] + 0.125 * total + 0.5 * drift)
    direct = kept * (1.0 - TRACER_RATE)
    h_out = [direct * value + common for value in q]
    sxy, dxy = s[4] + s[5], s[4] - s[5]
    sxz, dxz = s[6] + s[7], s[6] - s[7]
    syz, dyz = s[8] + s[9], s[8] - s[9]
    axis_sum = (s[1] + s[2]) + s[3]
    edge_sum = (sxy + sxz) + syz
    ce, cs = 1.19 / 2394.0, 1.4 / 252.0
    te = (8.0 * ce) * edge_sum - (11.0 * ce) * axis_sum - (30.0 * ce) * p[0]
    ts = cs * edge_sum - (4.0 * cs) * axis_sum + (12.0 * cs) * p[0]
    rx, ry, rz = s[1] - syz, s[2] - sxz, s[3] - sxy
    r_third = (axis_sum - edge_sum) * (1.0 / 3.0)
    gx, gy, gz = 2.0 * s[1] + syz, 2.0 * s[2] + sxz, 2.0 * s[3] + sxy
    g_third = (2.0 * axis_sum + edge_sum) * (1.0 / 3.0)
    cp, cq = 1.25 * 6.0 / 36.0, 1.4 * 6.0 / 72.0
    px, py, pz = cp * (rx - r_third), cp * (ry - r_third), cp * (rz - r_third)
    wx, wy, wz = cq * (gx - g_third), cq * (gy - g_third), cq * (gz - g_third)
    txy, txz, tyz = (1.25 / 4.0) * dxy, (1.25 / 4.0) * dxz, (1.25 / 4.0) * dyz
    base = 38.0 * te - 11.0 * ts
    sx = base + 2.0 * px + wx
    sy = base + 2.0 * py + wy
    sz = base + 2.0 * pz + wz
    vx = sx * ux + txy * uy + txz * uz
    vy = txy * ux + sy * uy + tyz * uz
    vz = txz * ux + tyz * uy + sz * uz
    nx, ny, nz = vx + bx, vy + by, vz + bz
    shift = ux * (nx - 0.5 * vx) + uy * (ny - 0.5 * vy) + uz * (nz - 0.5 * vz)
    e0 = 9.0 * ts - 19.0 * te + shift
    ea = shift - 7.0 * ts
    ee = 19.0 * te - 2.0 * ts + shift
    even_axis = [ea + px + 2.0 * wx, ea + py + 2.0 * wy, ea + pz + 2.0 * wz]
    exy, exz, eyz = ee - pz + wz, ee - py + wy, ee - px + wx
    axy, bxy = d[4] + d[5], d[4] - d[5]
    axz, bxz = d[6] + d[7], d[6] - d[7]
    ayz, byz = d[8] + d[9], d[8] - d[9]
    ck, cm = 1.2 / 40.0, 1.98 / 8.0
    kx = ck * ((axy + axz) - 4.0 * d[1])
    ky = ck * ((bxy + ayz) - 4.0 * d[2])
    kz = ck * ((bxz + byz) - 4.0 * d[3])
    mx, my, mz = cm * (axy - axz), cm * (ayz - bxy), cm * (bxz - byz)
    jx, jy, jz = (5.0 / 3.0) * kx - nx, (5.0 / 3.0) * ky - ny, (5.0 / 3.0) * kz - nz
    odd_axis = [jx - 5.0 * kx, jy - 5.0 * ky, jz - 5.0 * kz]
    xp, xm, yp, ym, zp, zm = jx + mx, jx - mx, jy + my, jy - my, jz + mz, jz - mz
    even = even_axis + [exy + txy, exy - txy, exz + txz, exz - txz, eyz + tyz, eyz - tyz]
    odd = odd_axis + [xp + ym, xp - ym, xm + zp, xm - zp, yp + zm, yp - zm]
    solid = label == 1
    f_out = [jnp.where(solid, p[0], p[0] - e0)]
    for k in range(9):
        up, down = p[2 * k + 1], p[2 * k + 2]
        f_out.append(jnp.where(solid, down, up - (even[k] + odd[k])))
        f_out.append(jnp.where(solid, up, down - (even[k] - odd[k])))
    h_final = [jnp.where(solid, q[0], h_out[0])]
    for k in range(3):
        h_final.append(jnp.where(solid, q[2 * k + 2], h_out[2 * k + 1]))
        h_final.append(jnp.where(solid, q[2 * k + 1], h_out[2 * k + 2]))
    return f_out, h_final


def tiles(rows, lanes):
    lane = lax.broadcasted_iota(jnp.int32, (rows, lanes), 1)
    row = lax.broadcasted_iota(jnp.int32, (rows, lanes), 0)
    return lane, [lane == 0, lane == lanes - 1], [row == rows - 1, row == 0]


def pull_plane(z, field, halo_x, got, ends, edges):
    planes, rows, lanes = field.shape[1:]
    pulled = []
    for number in range(COUNT):
        cx, cy, cz = SPEEDS[number]
        zz = lax.rem(z + (cz + planes), planes) if cz else z
        value = field[number, zz]
        if cy:
            side = 0 if cy == 1 else 1
            at = (SLOT * cz) % lanes + Y_LISTS[side].index(number)
            to = 0 if cy == 1 else lanes - 1
            column = pltpu.roll(got[side], (to - at) % lanes, 1)
            value = jnp.where(ends[side], column, value)
        if cx:
            side = 0 if cx == 1 else 1
            k = X_LISTS[side].index(number)
            value = pltpu.roll(value, rows - 1 if cx == 1 else 1, 0)
            halo = jnp.broadcast_to(halo_x[side, k, pl.ds(zz, 1), :], (rows, lanes))
            value = jnp.where(edges[side], halo, value)
        if cy:
            value = pltpu.roll(value, lanes - 1 if cy == 1 else 1, 1)
        pulled.append(value)
    return pulled


def kernel(
    sf_hbm, st_hbm, af_hbm, at_hbm, lab_hbm,
    field_out, macro_out, halo_x_out, halo_y_out, lab,
    sf, st, field, macro, send_x, recv_x, send_y, recv_y, recv_c,
    in_sem, send_sem, recv_sem,
):
    nx, ny = lax.axis_size("gx"), lax.axis_size("gy")
    mx, my = lax.axis_index("gx"), lax.axis_index("gy")
    steps, planes = sf.shape[0], sf.shape[2]
    rows, lanes = sf.shape[3], sf.shape[4]
    flow = sf.shape[1]
    x_next, x_prior = lax.rem(mx + 1, nx), lax.rem(mx + nx - 1, nx)
    y_next, y_prior = lax.rem(my + 1, ny), lax.rem(my + ny - 1, ny)
    neighbours = [
        (x_prior, my), (x_next, my), (mx, y_prior), (mx, y_next),
        (x_prior, y_prior), (x_next, y_next), (x_prior, y_next), (x_next, y_prior),
    ]
    barrier = pltpu.get_barrier_semaphore()
    for device in neighbours:
        pl.semaphore_signal(barrier, inc=1, device_id=device, device_id_type=MESH)

    loads = [
        pltpu.make_async_copy(af_hbm, field.at[0, pl.ds(0, flow)], in_sem.at[0]),
        pltpu.make_async_copy(at_hbm, field.at[0, pl.ds(flow, COUNT - flow)], in_sem.at[1]),
        pltpu.make_async_copy(sf_hbm, sf, in_sem.at[2]),
        pltpu.make_async_copy(st_hbm, st, in_sem.at[3]),
        pltpu.make_async_copy(lab_hbm, lab, in_sem.at[4]),
    ]
    for load in loads:
        load.start()

    lane, ends, edges = tiles(rows, lanes)
    def insert(packed, values):
        done = []
        for side in range(2):
            acc = pltpu.roll(packed[side], lanes - SLOT, 1)
            for k, number in enumerate(Y_LISTS[side]):
                target = lanes - SLOT + k
                moved = pltpu.roll(values[number], target + side, 1)
                acc = jnp.where(lane == target, moved, acc)
            done.append(acc)
        return tuple(done)

    def send(step, source):
        for side in range(2):
            at = 0 if side == 0 else rows - 1
            for k, number in enumerate(X_LISTS[side]):
                send_x[step, side, k] = source[number, :, at, :]
        pairs = [
            (send_x.at[step, 0], recv_x.at[step, 0]),
            (send_x.at[step, 1], recv_x.at[step, 1]),
            (send_y.at[step, 0], recv_y.at[step, 0]),
            (send_y.at[step, 1], recv_y.at[step, 1]),
            (send_x.at[step, 0, 1], recv_c.at[step, 0]),
            (send_x.at[step, 1, 1], recv_c.at[step, 1]),
            (send_x.at[step, 0, 2], recv_c.at[step, 2]),
            (send_x.at[step, 1, 2], recv_c.at[step, 3]),
        ]
        copies = []
        for number, ((source_ref, target_ref), device) in enumerate(zip(pairs, neighbours)):
            copies.append(
                pltpu.make_async_remote_copy(
                    src_ref=source_ref,
                    dst_ref=target_ref,
                    send_sem=send_sem.at[step, number],
                    recv_sem=recv_sem.at[step, number],
                    device_id=device,
                    device_id_type=MESH,
                )
            )
        for copy in copies:
            copy.start()
        return copies

    loads[0].wait()
    loads[1].wait()

    def first_pack(z, packed):
        values = {n: field[0, n, z] for side in Y_LISTS for n in side}
        return insert(packed, values)

    empty = (jnp.zeros((rows, lanes), jnp.float32),) * 2
    packed = lax.fori_loop(0, planes, first_pack, empty, unroll=8)
    send_y[0, 0] = packed[0]
    send_y[0, 1] = packed[1]
    pl.semaphore_wait(barrier, len(neighbours))
    started = [send(0, field.at[0])]
    for load in loads[2:]:
        load.wait()

    def prepare(index, carry):
        step, z = index // planes, index % planes
        f = [sf[step, n, z].astype(jnp.float32) for n in range(flow)]
        h = [st[step, n, z].astype(jnp.float32) for n in range(COUNT - flow)]
        for k, value in enumerate(macros(f, h)):
            macro[step, k, z] = value
        return carry

    lax.fori_loop(0, steps * planes, prepare, 0, unroll=4)
    macro_out[...] = macro[0]

    buffers = [field.at[step % 2] for step in range(steps - 1)] + [field_out]

    for step in range(steps):
        saved = steps - 1 - step
        source = buffers[step]
        for copy in started[step]:
            copy.wait_recv()
        for corner, number in enumerate(CORNERS):
            side = 0 if SPEEDS[number][0] == 1 else 1
            end = ends[0] if SPEEDS[number][1] == 1 else ends[1]
            k = X_LISTS[side].index(number)
            recv_x[step, side, k] = jnp.where(end, recv_c[step, corner], recv_x[step, side, k])
        if step == steps - 1:
            halo_x_out[...] = recv_x[step]
            halo_y_out[...] = recv_y[step]
            break
        target = buffers[step + 1]
        halo_x = recv_x.at[step]

        def plane(z, carry):
            got, packed = carry
            pulled = pull_plane(z, source, halo_x, got, ends, edges)
            ux, uy, uz, cr = [macro[saved, k, z] for k in range(4)]
            f_out, h_out = transpose_collision(
                pulled[:flow], pulled[flow:], ux, uy, uz, cr, lab[z]
            )
            values = f_out + h_out
            for number in range(COUNT):
                target[number, z] = values[number]
            got = tuple(pltpu.roll(value, lanes - SLOT, 1) for value in got)
            return got, insert(packed, values)

        got = (recv_y[step, 0], recv_y[step, 1])
        got, packed = lax.fori_loop(0, planes, plane, (got, empty), unroll=8)
        send_y[step + 1, 0] = packed[0]
        send_y[step + 1, 1] = packed[1]
        started.append(send(step + 1, target))
    for copies in started:
        for copy in copies:
            copy.wait_send()


def finish(field, macro, halo_x, halo_y, lab, of_hbm, ot_hbm, stage, out_sem):
    planes, rows, lanes = field.shape[1:]
    flow = of_hbm.shape[0]
    _, ends, edges = tiles(rows, lanes)

    def stores(z):
        return [
            pltpu.make_async_copy(
                stage.at[pl.ds(0, flow), z], of_hbm.at[:, z], out_sem.at[0, z]
            ),
            pltpu.make_async_copy(
                stage.at[pl.ds(flow, COUNT - flow), z], ot_hbm.at[:, z], out_sem.at[1, z]
            ),
        ]

    got = (halo_y[0], halo_y[1])
    for z in range(planes):
        pulled = pull_plane(z, field, halo_x, got, ends, edges)
        ux, uy, uz, cr = [macro[k, z] for k in range(4)]
        f_out, h_out = transpose_collision(
            pulled[:flow], pulled[flow:], ux, uy, uz, cr, lab[z]
        )
        for number, value in enumerate(f_out + h_out):
            stage[number, z] = value
        for store in stores(z):
            store.start()
        got = tuple(pltpu.roll(value, lanes - SLOT, 1) for value in got)
    for z in range(planes):
        for store in stores(z):
            store.wait()


def body(saved_fluid, saved_tracer, adjoint_fluid, adjoint_tracer, label):
    steps, flow, planes, rows, lanes = saved_fluid.shape
    tracer = saved_tracer.shape[1]
    f32 = jnp.float32
    tile = (rows, lanes)
    whole = (flow + tracer, planes) + tile
    vmem, hbm = pl.BlockSpec(memory_space=pltpu.VMEM), pl.BlockSpec(memory_space=IN_SPACE)
    ready = pl.pallas_call(
        kernel,
        out_shape=(
            jax.ShapeDtypeStruct(whole, f32),
            jax.ShapeDtypeStruct((4, planes) + tile, f32),
            jax.ShapeDtypeStruct((2, 6, planes, lanes), f32),
            jax.ShapeDtypeStruct((2,) + tile, f32),
            jax.ShapeDtypeStruct(label.shape, label.dtype),
        ),
        in_specs=[hbm] * 5,
        out_specs=[vmem] * 5,
        scratch_shapes=[
            pltpu.VMEM(saved_fluid.shape, saved_fluid.dtype),
            pltpu.VMEM(saved_tracer.shape, saved_tracer.dtype),
            pltpu.VMEM((2,) + whole, f32),
            pltpu.VMEM((steps, 4, planes) + tile, f32),
            pltpu.VMEM((steps, 2, 6, planes, lanes), f32),
            pltpu.VMEM((steps, 2, 6, planes, lanes), f32),
            pltpu.VMEM((steps, 2) + tile, f32),
            pltpu.VMEM((steps, 2) + tile, f32),
            pltpu.VMEM((steps, 4, planes, lanes), f32),
            pltpu.SemaphoreType.DMA((5,)),
            pltpu.SemaphoreType.DMA((steps, 8)),
            pltpu.SemaphoreType.DMA((steps, 8)),
        ],
        compiler_params=pltpu.CompilerParams(
            collective_id=0, has_side_effects=True, vmem_limit_bytes=FIRST_VMEM
        ),
        name="adjoint_steps",
    )(*[pltpu.with_memory_space_constraint(value, pltpu.HBM) for value in (saved_fluid, saved_tracer, adjoint_fluid, adjoint_tracer, label)])
    return pl.pallas_call(
        finish,
        out_shape=(
            jax.ShapeDtypeStruct(adjoint_fluid.shape, f32),
            jax.ShapeDtypeStruct(adjoint_tracer.shape, f32),
        ),
        in_specs=[vmem] * 5,
        out_specs=[pl.BlockSpec(memory_space=pl.ANY)] * 2,
        scratch_shapes=[
            pltpu.VMEM(whole, f32),
            pltpu.SemaphoreType.DMA((2, planes)),
        ],
        compiler_params=pltpu.CompilerParams(vmem_limit_bytes=16 * 1024 * 1024),
        name="last_step",
    )(*ready)


def solution(mesh):
    placed = (
        P(None, None, None, "gx", "gy"),
        P(None, None, None, "gx", "gy"),
        P(None, None, "gx", "gy"),
        P(None, None, "gx", "gy"),
        P(None, "gx", "gy"),
    )
    return jax.shard_map(
        body,
        mesh=mesh,
        in_specs=placed,
        out_specs=(P(None, None, "gx", "gy"), P(None, None, "gx", "gy")),
        check_vma=False,
    )
```

```python
import functools

import jax
import jax.numpy as jnp
from jax import lax
from jax.experimental import pallas as pl
from jax.experimental.pallas import tpu as pltpu
from jax.sharding import PartitionSpec as P

TRACER_RATE = 1.3
ADSORB = 0.3
FLOW = [
    (0, 0, 0), (1, 0, 0), (-1, 0, 0), (0, 1, 0), (0, -1, 0), (0, 0, 1), (0, 0, -1),
    (1, 1, 0), (-1, -1, 0), (1, -1, 0), (-1, 1, 0), (1, 0, 1), (-1, 0, -1), (1, 0, -1),
    (-1, 0, 1), (0, 1, 1), (0, -1, -1), (0, 1, -1), (0, -1, 1),
]
SPEEDS = FLOW + FLOW[:7]
COUNT = len(SPEEDS)
X_LISTS = [[1, 7, 9, 11, 13, 20], [2, 8, 10, 12, 14, 21]]
Y_LISTS = [[3, 7, 10, 15, 17, 22], [4, 8, 9, 16, 18, 23]]
CORNERS = [7, 8, 9, 10]
MESH = pl.DeviceIdType.MESH
SLOT = 16
IN_SPACE = pltpu.HBM
FIRST_VMEM = 32 * 1024 * 1024


def macros(f, h):
    s = [f[2 * k - 1] + f[2 * k] for k in range(1, 10)]
    d = [f[2 * k - 1] - f[2 * k] for k in range(1, 10)]
    rho = f[0] + ((s[0] + s[1]) + (s[2] + s[3])) + ((s[4] + s[5]) + (s[6] + s[7])) + s[8]
    inv = 1.0 / rho
    ux = (d[0] + (d[3] + d[4]) + (d[5] + d[6])) * inv
    uy = (d[1] + (d[3] - d[4]) + (d[7] + d[8])) * inv
    uz = (d[2] + (d[5] - d[6]) + (d[7] - d[8])) * inv
    amount = h[0] + ((h[1] + h[2]) + (h[3] + h[4])) + (h[5] + h[6])
    return ux, uy, uz, amount * inv * (4.0 * TRACER_RATE * 0.125)


def transpose_collision(p, q, ux, uy, uz, cr, label):
    s = [None] + [p[2 * k - 1] + p[2 * k] for k in range(1, 10)]
    d = [None] + [p[2 * k - 1] - p[2 * k] for k in range(1, 10)]
    kept = jnp.where(label == 2, 1.0 - ADSORB, 1.0)
    tx, ty, tz = q[1] - q[2], q[3] - q[4], q[5] - q[6]
    crk = cr * kept
    bx, by, bz = crk * tx, crk * ty, crk * tz
    total = ((q[1] + q[2]) + (q[3] + q[4])) + (q[5] + q[6])
    drift = ux * tx + uy * ty + uz * tz
    common = (kept * TRACER_RATE) * (0.25 * q[0] + 0.125 * total + 0.5 * drift)
    direct = kept * (1.0 - TRACER_RATE)
    h_out = [direct * value + common for value in q]
    sxy, dxy = s[4] + s[5], s[4] - s[5]
    sxz, dxz = s[6] + s[7], s[6] - s[7]
    syz, dyz = s[8] + s[9], s[8] - s[9]
    axis_sum = (s[1] + s[2]) + s[3]
    edge_sum = (sxy + sxz) + syz
    ce, cs = 1.19 / 2394.0, 1.4 / 252.0
    te = (8.0 * ce) * edge_sum - (11.0 * ce) * axis_sum - (30.0 * ce) * p[0]
    ts = cs * edge_sum - (4.0 * cs) * axis_sum + (12.0 * cs) * p[0]
    rx, ry, rz = s[1] - syz, s[2] - sxz, s[3] - sxy
    r_third = (axis_sum - edge_sum) * (1.0 / 3.0)
    gx, gy, gz = 2.0 * s[1] + syz, 2.0 * s[2] + sxz, 2.0 * s[3] + sxy
    g_third = (2.0 * axis_sum + edge_sum) * (1.0 / 3.0)
    cp, cq = 1.25 * 6.0 / 36.0, 1.4 * 6.0 / 72.0
    px, py, pz = cp * (rx - r_third), cp * (ry - r_third), cp * (rz - r_third)
    wx, wy, wz = cq * (gx - g_third), cq * (gy - g_third), cq * (gz - g_third)
    txy, txz, tyz = (1.25 / 4.0) * dxy, (1.25 / 4.0) * dxz, (1.25 / 4.0) * dyz
    base = 38.0 * te - 11.0 * ts
    sx = base + 2.0 * px + wx
    sy = base + 2.0 * py + wy
    sz = base + 2.0 * pz + wz
    vx = sx * ux + txy * uy + txz * uz
    vy = txy * ux + sy * uy + tyz * uz
    vz = txz * ux + tyz * uy + sz * uz
    nx, ny, nz = vx + bx, vy + by, vz + bz
    shift = ux * (nx - 0.5 * vx) + uy * (ny - 0.5 * vy) + uz * (nz - 0.5 * vz)
    e0 = 9.0 * ts - 19.0 * te + shift
    ea = shift - 7.0 * ts
    ee = 19.0 * te - 2.0 * ts + shift
    even_axis = [ea + px + 2.0 * wx, ea + py + 2.0 * wy, ea + pz + 2.0 * wz]
    exy, exz, eyz = ee - pz + wz, ee - py + wy, ee - px + wx
    axy, bxy = d[4] + d[5], d[4] - d[5]
    axz, bxz = d[6] + d[7], d[6] - d[7]
    ayz, byz = d[8] + d[9], d[8] - d[9]
    ck, cm = 1.2 / 40.0, 1.98 / 8.0
    kx = ck * ((axy + axz) - 4.0 * d[1])
    ky = ck * ((bxy + ayz) - 4.0 * d[2])
    kz = ck * ((bxz + byz) - 4.0 * d[3])
    mx, my, mz = cm * (axy - axz), cm * (ayz - bxy), cm * (bxz - byz)
    jx, jy, jz = (5.0 / 3.0) * kx - nx, (5.0 / 3.0) * ky - ny, (5.0 / 3.0) * kz - nz
    odd_axis = [jx - 5.0 * kx, jy - 5.0 * ky, jz - 5.0 * kz]
    xp, xm, yp, ym, zp, zm = jx + mx, jx - mx, jy + my, jy - my, jz + mz, jz - mz
    even = even_axis + [exy + txy, exy - txy, exz + txz, exz - txz, eyz + tyz, eyz - tyz]
    odd = odd_axis + [xp + ym, xp - ym, xm + zp, xm - zp, yp + zm, yp - zm]
    solid = label == 1
    f_out = [jnp.where(solid, p[0], p[0] - e0)]
    for k in range(9):
        up, down = p[2 * k + 1], p[2 * k + 2]
        f_out.append(jnp.where(solid, down, up - (even[k] + odd[k])))
        f_out.append(jnp.where(solid, up, down - (even[k] - odd[k])))
    h_final = [jnp.where(solid, q[0], h_out[0])]
    for k in range(3):
        h_final.append(jnp.where(solid, q[2 * k + 2], h_out[2 * k + 1]))
        h_final.append(jnp.where(solid, q[2 * k + 1], h_out[2 * k + 2]))
    return f_out, h_final


def tiles(rows, lanes):
    lane = lax.broadcasted_iota(jnp.int32, (rows, lanes), 1)
    row = lax.broadcasted_iota(jnp.int32, (rows, lanes), 0)
    return lane, [lane == 0, lane == lanes - 1], [row == rows - 1, row == 0]


def turn(value, cx, cy, rows, lanes):
    if cx:
        value = pltpu.roll(value, rows - 1 if cx == 1 else 1, 0)
    if cy:
        value = pltpu.roll(value, lanes - 1 if cy == 1 else 1, 1)
    return value


def pull_plane(z, field, halo_x, got, ends, edges):
    planes, rows, lanes = field.shape[1:]
    pulled = []
    for number in range(COUNT):
        cx, cy, cz = SPEEDS[number]
        zz = lax.rem(z + (cz + planes), planes) if cz else z
        value = field[number, zz]
        if cy:
            side = 0 if cy == 1 else 1
            at = (SLOT * cz) % lanes + Y_LISTS[side].index(number)
            to = lanes - 1 if cy == 1 else 0
            column = turn(pltpu.roll(got[side], (to - at) % lanes, 1), cx, 0, rows, lanes)
            value = jnp.where(ends[1 - side], column, value)
        if cx:
            side = 0 if cx == 1 else 1
            k = X_LISTS[side].index(number)
            halo = jnp.broadcast_to(halo_x[side, k, pl.ds(zz, 1), :], (rows, lanes))
            value = jnp.where(edges[side], halo, value)
        pulled.append(value)
    return pulled


def kernel(
    sf_hbm, st_hbm, af_hbm, at_hbm, lab_hbm,
    field_out, macro_out, halo_x_out, halo_y_out, lab,
    sf, st, field, macro, send_x, recv_x, send_y, recv_y, recv_c,
    in_sem, send_sem, recv_sem,
):
    nx, ny = lax.axis_size("gx"), lax.axis_size("gy")
    mx, my = lax.axis_index("gx"), lax.axis_index("gy")
    steps, planes = sf.shape[0], sf.shape[2]
    rows, lanes = sf.shape[3], sf.shape[4]
    flow = sf.shape[1]
    x_next, x_prior = lax.rem(mx + 1, nx), lax.rem(mx + nx - 1, nx)
    y_next, y_prior = lax.rem(my + 1, ny), lax.rem(my + ny - 1, ny)
    neighbours = [
        (x_prior, my), (x_next, my), (mx, y_prior), (mx, y_next),
        (x_prior, y_prior), (x_next, y_next), (x_prior, y_next), (x_next, y_prior),
    ]
    barrier = pltpu.get_barrier_semaphore()
    for device in neighbours[4:] + neighbours[:4]:
        pl.semaphore_signal(barrier, inc=1, device_id=device, device_id_type=MESH)

    loads = [
        pltpu.make_async_copy(af_hbm, field.at[0, pl.ds(0, flow)], in_sem.at[0]),
        pltpu.make_async_copy(at_hbm, field.at[0, pl.ds(flow, COUNT - flow)], in_sem.at[1]),
        pltpu.make_async_copy(sf_hbm, sf, in_sem.at[2]),
        pltpu.make_async_copy(st_hbm, st, in_sem.at[3]),
        pltpu.make_async_copy(lab_hbm, lab, in_sem.at[4]),
    ]
    for load in loads[:2]:
        load.start()

    lane, ends, edges = tiles(rows, lanes)
    def insert(packed, values):
        done = []
        for side in range(2):
            acc = pltpu.roll(packed[side], lanes - SLOT, 1)
            for k, number in enumerate(Y_LISTS[side]):
                target = lanes - SLOT + k
                moved = pltpu.roll(values[number], target + side, 1)
                acc = jnp.where(lane == target, moved, acc)
            done.append(acc)
        return tuple(done)

    def send(step, source):
        def face(slots):
            for side in range(2):
                at = 0 if side == 0 else rows - 1
                for k in slots:
                    send_x[step, side, k] = source[X_LISTS[side][k], :, at, :]

        pairs = [
            (send_x.at[step, 0], recv_x.at[step, 0]),
            (send_x.at[step, 1], recv_x.at[step, 1]),
            (send_y.at[step, 0], recv_y.at[step, 0]),
            (send_y.at[step, 1], recv_y.at[step, 1]),
            (send_x.at[step, 0, 1], recv_c.at[step, 0]),
            (send_x.at[step, 1, 1], recv_c.at[step, 1]),
            (send_x.at[step, 0, 2], recv_c.at[step, 2]),
            (send_x.at[step, 1, 2], recv_c.at[step, 3]),
        ]
        copies = [
            pltpu.make_async_remote_copy(
                src_ref=source_ref,
                dst_ref=target_ref,
                send_sem=send_sem.at[step, number],
                recv_sem=recv_sem.at[step, number],
                device_id=device,
                device_id_type=MESH,
            )
            for number, ((source_ref, target_ref), device) in enumerate(zip(pairs, neighbours))
        ]
        face((1, 2))
        for copy in copies[4:] + copies[2:4]:
            copy.start()
        face((0, 3, 4, 5))
        for copy in copies[:2]:
            copy.start()
        return copies

    loads[0].wait()
    loads[1].wait()
    for load in loads[2:]:
        load.start()

    def first_pack(z, packed):
        values = {n: field[0, n, z] for side in Y_LISTS for n in side}
        return insert(packed, values)

    empty = (jnp.zeros((rows, lanes), jnp.float32),) * 2
    packed = lax.fori_loop(0, planes, first_pack, empty, unroll=8)
    send_y[0, 0] = packed[0]
    send_y[0, 1] = packed[1]
    pl.semaphore_wait(barrier, len(neighbours))
    started = [send(0, field.at[0])]
    for load in loads[2:]:
        load.wait()

    def prepare(index, carry):
        step, z = index // planes, index % planes
        f = [sf[step, n, z].astype(jnp.float32) for n in range(flow)]
        h = [st[step, n, z].astype(jnp.float32) for n in range(COUNT - flow)]
        for k, value in enumerate(macros(f, h)):
            macro[step, k, z] = value
        return carry

    lax.fori_loop(0, steps * planes, prepare, 0, unroll=4)
    macro_out[...] = macro[0]

    buffers = [field.at[step % 2] for step in range(steps - 1)] + [field_out]

    for step in range(steps):
        saved = steps - 1 - step
        source = buffers[step]

        def turn_plane(z, carry):
            for number in range(COUNT):
                cx, cy, _ = SPEEDS[number]
                if cx or cy:
                    source[number, z] = turn(source[number, z], cx, cy, rows, lanes)
            return carry

        lax.fori_loop(0, planes, turn_plane, 0, unroll=2)
        for copy in started[step]:
            copy.wait_recv()
        for corner, number in enumerate(CORNERS):
            side = 0 if SPEEDS[number][0] == 1 else 1
            end = ends[0] if SPEEDS[number][1] == 1 else ends[1]
            k = X_LISTS[side].index(number)
            merged = jnp.where(end, recv_c[step, corner], recv_x[step, side, k])
            recv_x[step, side, k] = turn(merged, 0, SPEEDS[number][1], rows, lanes)
        if step == steps - 1:
            halo_x_out[...] = recv_x[step]
            halo_y_out[...] = recv_y[step]
            break
        target = buffers[step + 1]
        halo_x = recv_x.at[step]

        def plane(z, carry):
            got, packed = carry
            pulled = pull_plane(z, source, halo_x, got, ends, edges)
            ux, uy, uz, cr = [macro[saved, k, z] for k in range(4)]
            f_out, h_out = transpose_collision(
                pulled[:flow], pulled[flow:], ux, uy, uz, cr, lab[z]
            )
            values = f_out + h_out
            for number in range(COUNT):
                target[number, z] = values[number]
            got = tuple(pltpu.roll(value, lanes - SLOT, 1) for value in got)
            return got, insert(packed, values)

        got = (recv_y[step, 0], recv_y[step, 1])
        got, packed = lax.fori_loop(0, planes, plane, (got, empty), unroll=8)
        send_y[step + 1, 0] = packed[0]
        send_y[step + 1, 1] = packed[1]
        started.append(send(step + 1, target))
    for copies in started:
        for copy in copies:
            copy.wait_send()


def finish(field, macro, halo_x, halo_y, lab, of_hbm, ot_hbm, stage, out_sem):
    planes, rows, lanes = field.shape[1:]
    flow = of_hbm.shape[0]
    _, ends, edges = tiles(rows, lanes)

    def stores(z):
        return [
            pltpu.make_async_copy(
                stage.at[pl.ds(0, flow), z], of_hbm.at[:, z], out_sem.at[0, z]
            ),
            pltpu.make_async_copy(
                stage.at[pl.ds(flow, COUNT - flow), z], ot_hbm.at[:, z], out_sem.at[1, z]
            ),
        ]

    got = (halo_y[0], halo_y[1])
    for z in range(planes):
        pulled = pull_plane(z, field, halo_x, got, ends, edges)
        ux, uy, uz, cr = [macro[k, z] for k in range(4)]
        f_out, h_out = transpose_collision(
            pulled[:flow], pulled[flow:], ux, uy, uz, cr, lab[z]
        )
        for number, value in enumerate(f_out + h_out):
            stage[number, z] = value
        for store in stores(z):
            store.start()
        got = tuple(pltpu.roll(value, lanes - SLOT, 1) for value in got)
    for z in range(planes):
        for store in stores(z):
            store.wait()


def body(saved_fluid, saved_tracer, adjoint_fluid, adjoint_tracer, label):
    steps, flow, planes, rows, lanes = saved_fluid.shape
    tracer = saved_tracer.shape[1]
    f32 = jnp.float32
    tile = (rows, lanes)
    whole = (flow + tracer, planes) + tile
    vmem, hbm = pl.BlockSpec(memory_space=pltpu.VMEM), pl.BlockSpec(memory_space=IN_SPACE)
    ready = pl.pallas_call(
        kernel,
        out_shape=(
            jax.ShapeDtypeStruct(whole, f32),
            jax.ShapeDtypeStruct((4, planes) + tile, f32),
            jax.ShapeDtypeStruct((2, 6, planes, lanes), f32),
            jax.ShapeDtypeStruct((2,) + tile, f32),
            jax.ShapeDtypeStruct(label.shape, label.dtype),
        ),
        in_specs=[hbm] * 5,
        out_specs=[vmem] * 5,
        scratch_shapes=[
            pltpu.VMEM(saved_fluid.shape, saved_fluid.dtype),
            pltpu.VMEM(saved_tracer.shape, saved_tracer.dtype),
            pltpu.VMEM((2,) + whole, f32),
            pltpu.VMEM((steps, 4, planes) + tile, f32),
            pltpu.VMEM((steps, 2, 6, planes, lanes), f32),
            pltpu.VMEM((steps, 2, 6, planes, lanes), f32),
            pltpu.VMEM((steps, 2) + tile, f32),
            pltpu.VMEM((steps, 2) + tile, f32),
            pltpu.VMEM((steps, 4, planes, lanes), f32),
            pltpu.SemaphoreType.DMA((5,)),
            pltpu.SemaphoreType.DMA((steps, 8)),
            pltpu.SemaphoreType.DMA((steps, 8)),
        ],
        compiler_params=pltpu.CompilerParams(
            collective_id=0, has_side_effects=True, vmem_limit_bytes=FIRST_VMEM
        ),
        name="adjoint_steps",
    )(*[pltpu.with_memory_space_constraint(value, pltpu.HBM) for value in (saved_fluid, saved_tracer, adjoint_fluid, adjoint_tracer, label)])
    return pl.pallas_call(
        finish,
        out_shape=(
            jax.ShapeDtypeStruct(adjoint_fluid.shape, f32),
            jax.ShapeDtypeStruct(adjoint_tracer.shape, f32),
        ),
        in_specs=[vmem] * 5,
        out_specs=[pl.BlockSpec(memory_space=pl.ANY)] * 2,
        scratch_shapes=[
            pltpu.VMEM(whole, f32),
            pltpu.SemaphoreType.DMA((2, planes)),
        ],
        compiler_params=pltpu.CompilerParams(vmem_limit_bytes=16 * 1024 * 1024),
        name="last_step",
    )(*ready)


def solution(mesh):
    placed = (
        P(None, None, None, "gx", "gy"),
        P(None, None, None, "gx", "gy"),
        P(None, None, "gx", "gy"),
        P(None, None, "gx", "gy"),
        P(None, "gx", "gy"),
    )
    return jax.shard_map(
        body,
        mesh=mesh,
        in_specs=placed,
        out_specs=(P(None, None, "gx", "gy"), P(None, None, "gx", "gy")),
        check_vma=False,
    )
```

```python
import functools

import jax
import jax.numpy as jnp
from jax import lax
from jax.experimental import pallas as pl
from jax.experimental.pallas import tpu as pltpu
from jax.sharding import PartitionSpec as P

TRACER_RATE = 1.3
ADSORB = 0.3
FLOW = [
    (0, 0, 0), (1, 0, 0), (-1, 0, 0), (0, 1, 0), (0, -1, 0), (0, 0, 1), (0, 0, -1),
    (1, 1, 0), (-1, -1, 0), (1, -1, 0), (-1, 1, 0), (1, 0, 1), (-1, 0, -1), (1, 0, -1),
    (-1, 0, 1), (0, 1, 1), (0, -1, -1), (0, 1, -1), (0, -1, 1),
]
SPEEDS = FLOW + FLOW[:7]
COUNT = len(SPEEDS)
X_LISTS = [[1, 7, 9, 11, 13, 20], [2, 8, 10, 12, 14, 21]]
Y_LISTS = [[3, 7, 10, 15, 17, 22], [4, 8, 9, 16, 18, 23]]
CORNERS = [7, 8, 9, 10]
MESH = pl.DeviceIdType.MESH
SLOT = 16
IN_SPACE = pltpu.HBM
FIRST_VMEM = 32 * 1024 * 1024


def macros(f, h):
    s = [f[2 * k - 1] + f[2 * k] for k in range(1, 10)]
    d = [f[2 * k - 1] - f[2 * k] for k in range(1, 10)]
    rho = f[0] + ((s[0] + s[1]) + (s[2] + s[3])) + ((s[4] + s[5]) + (s[6] + s[7])) + s[8]
    inv = 1.0 / rho
    ux = (d[0] + (d[3] + d[4]) + (d[5] + d[6])) * inv
    uy = (d[1] + (d[3] - d[4]) + (d[7] + d[8])) * inv
    uz = (d[2] + (d[5] - d[6]) + (d[7] - d[8])) * inv
    amount = h[0] + ((h[1] + h[2]) + (h[3] + h[4])) + (h[5] + h[6])
    return ux, uy, uz, amount * inv * (4.0 * TRACER_RATE * 0.125)


def transpose_collision(p, q, ux, uy, uz, cr, label):
    s = [None] + [p[2 * k - 1] + p[2 * k] for k in range(1, 10)]
    d = [None] + [p[2 * k - 1] - p[2 * k] for k in range(1, 10)]
    kept = jnp.where(label == 2, 1.0 - ADSORB, 1.0)
    tx, ty, tz = q[1] - q[2], q[3] - q[4], q[5] - q[6]
    crk = cr * kept
    bx, by, bz = crk * tx, crk * ty, crk * tz
    total = ((q[1] + q[2]) + (q[3] + q[4])) + (q[5] + q[6])
    drift = ux * tx + uy * ty + uz * tz
    common = (kept * TRACER_RATE) * (0.25 * q[0] + 0.125 * total + 0.5 * drift)
    direct = kept * (1.0 - TRACER_RATE)
    h_out = [direct * value + common for value in q]
    sxy, dxy = s[4] + s[5], s[4] - s[5]
    sxz, dxz = s[6] + s[7], s[6] - s[7]
    syz, dyz = s[8] + s[9], s[8] - s[9]
    axis_sum = (s[1] + s[2]) + s[3]
    edge_sum = (sxy + sxz) + syz
    ce, cs = 1.19 / 2394.0, 1.4 / 252.0
    te = (8.0 * ce) * edge_sum - (11.0 * ce) * axis_sum - (30.0 * ce) * p[0]
    ts = cs * edge_sum - (4.0 * cs) * axis_sum + (12.0 * cs) * p[0]
    rx, ry, rz = s[1] - syz, s[2] - sxz, s[3] - sxy
    r_third = (axis_sum - edge_sum) * (1.0 / 3.0)
    gx, gy, gz = 2.0 * s[1] + syz, 2.0 * s[2] + sxz, 2.0 * s[3] + sxy
    g_third = (2.0 * axis_sum + edge_sum) * (1.0 / 3.0)
    cp, cq = 1.25 * 6.0 / 36.0, 1.4 * 6.0 / 72.0
    px, py, pz = cp * (rx - r_third), cp * (ry - r_third), cp * (rz - r_third)
    wx, wy, wz = cq * (gx - g_third), cq * (gy - g_third), cq * (gz - g_third)
    txy, txz, tyz = (1.25 / 4.0) * dxy, (1.25 / 4.0) * dxz, (1.25 / 4.0) * dyz
    base = 38.0 * te - 11.0 * ts
    sx = base + 2.0 * px + wx
    sy = base + 2.0 * py + wy
    sz = base + 2.0 * pz + wz
    vx = sx * ux + txy * uy + txz * uz
    vy = txy * ux + sy * uy + tyz * uz
    vz = txz * ux + tyz * uy + sz * uz
    nx, ny, nz = vx + bx, vy + by, vz + bz
    shift = ux * (nx - 0.5 * vx) + uy * (ny - 0.5 * vy) + uz * (nz - 0.5 * vz)
    e0 = 9.0 * ts - 19.0 * te + shift
    ea = shift - 7.0 * ts
    ee = 19.0 * te - 2.0 * ts + shift
    even_axis = [ea + px + 2.0 * wx, ea + py + 2.0 * wy, ea + pz + 2.0 * wz]
    exy, exz, eyz = ee - pz + wz, ee - py + wy, ee - px + wx
    axy, bxy = d[4] + d[5], d[4] - d[5]
    axz, bxz = d[6] + d[7], d[6] - d[7]
    ayz, byz = d[8] + d[9], d[8] - d[9]
    ck, cm = 1.2 / 40.0, 1.98 / 8.0
    kx = ck * ((axy + axz) - 4.0 * d[1])
    ky = ck * ((bxy + ayz) - 4.0 * d[2])
    kz = ck * ((bxz + byz) - 4.0 * d[3])
    mx, my, mz = cm * (axy - axz), cm * (ayz - bxy), cm * (bxz - byz)
    jx, jy, jz = (5.0 / 3.0) * kx - nx, (5.0 / 3.0) * ky - ny, (5.0 / 3.0) * kz - nz
    odd_axis = [jx - 5.0 * kx, jy - 5.0 * ky, jz - 5.0 * kz]
    xp, xm, yp, ym, zp, zm = jx + mx, jx - mx, jy + my, jy - my, jz + mz, jz - mz
    even = even_axis + [exy + txy, exy - txy, exz + txz, exz - txz, eyz + tyz, eyz - tyz]
    odd = odd_axis + [xp + ym, xp - ym, xm + zp, xm - zp, yp + zm, yp - zm]
    solid = label == 1
    f_out = [jnp.where(solid, p[0], p[0] - e0)]
    for k in range(9):
        up, down = p[2 * k + 1], p[2 * k + 2]
        f_out.append(jnp.where(solid, down, up - (even[k] + odd[k])))
        f_out.append(jnp.where(solid, up, down - (even[k] - odd[k])))
    h_final = [jnp.where(solid, q[0], h_out[0])]
    for k in range(3):
        h_final.append(jnp.where(solid, q[2 * k + 2], h_out[2 * k + 1]))
        h_final.append(jnp.where(solid, q[2 * k + 1], h_out[2 * k + 2]))
    return f_out, h_final


def tiles(rows, lanes):
    lane = lax.broadcasted_iota(jnp.int32, (rows, lanes), 1)
    row = lax.broadcasted_iota(jnp.int32, (rows, lanes), 0)
    return lane, [lane == 0, lane == lanes - 1], [row == rows - 1, row == 0]


def turn(value, cx, cy, rows, lanes):
    if cx:
        value = pltpu.roll(value, rows - 1 if cx == 1 else 1, 0)
    if cy:
        value = pltpu.roll(value, lanes - 1 if cy == 1 else 1, 1)
    return value


def pull_plane(z, field, halo_x, got, ends, edges):
    planes, rows, lanes = field.shape[1:]
    pulled = []
    for number in range(COUNT):
        cx, cy, cz = SPEEDS[number]
        zz = lax.rem(z + (cz + planes), planes) if cz else z
        value = field[number, zz]
        if cy:
            side = 0 if cy == 1 else 1
            at = (SLOT * cz) % lanes + Y_LISTS[side].index(number)
            to = lanes - 1 if cy == 1 else 0
            column = turn(pltpu.roll(got[side], (to - at) % lanes, 1), cx, 0, rows, lanes)
            value = jnp.where(ends[1 - side], column, value)
        if cx:
            side = 0 if cx == 1 else 1
            k = X_LISTS[side].index(number)
            halo = jnp.broadcast_to(halo_x[side, k, pl.ds(zz, 1), :], (rows, lanes))
            value = jnp.where(edges[side], halo, value)
        pulled.append(value)
    return pulled


def kernel(
    sf_hbm, st_hbm, af_hbm, at_hbm, lab_hbm,
    field_out, macro_out, halo_x_out, halo_y_out, lab,
    sf, st, field, macro, send_x, recv_x, send_y, recv_y, recv_c,
    in_sem, send_sem, recv_sem,
):
    nx, ny = lax.axis_size("gx"), lax.axis_size("gy")
    mx, my = lax.axis_index("gx"), lax.axis_index("gy")
    steps, planes = sf.shape[0], sf.shape[2]
    rows, lanes = sf.shape[3], sf.shape[4]
    flow = sf.shape[1]
    x_next, x_prior = lax.rem(mx + 1, nx), lax.rem(mx + nx - 1, nx)
    y_next, y_prior = lax.rem(my + 1, ny), lax.rem(my + ny - 1, ny)
    neighbours = [
        (x_prior, my), (x_next, my), (mx, y_prior), (mx, y_next),
        (x_prior, y_prior), (x_next, y_next), (x_prior, y_next), (x_next, y_prior),
    ]
    barrier = pltpu.get_barrier_semaphore()
    for device in neighbours[4:] + neighbours[:4]:
        pl.semaphore_signal(barrier, inc=1, device_id=device, device_id_type=MESH)

    loads = [
        pltpu.make_async_copy(af_hbm, field.at[0, pl.ds(0, flow)], in_sem.at[0]),
        pltpu.make_async_copy(at_hbm, field.at[0, pl.ds(flow, COUNT - flow)], in_sem.at[1]),
        pltpu.make_async_copy(sf_hbm, sf, in_sem.at[2]),
        pltpu.make_async_copy(st_hbm, st, in_sem.at[3]),
        pltpu.make_async_copy(lab_hbm, lab, in_sem.at[4]),
    ]
    for load in loads[:2]:
        load.start()

    lane, ends, edges = tiles(rows, lanes)
    def insert(packed, values):
        done = []
        for side in range(2):
            acc = pltpu.roll(packed[side], lanes - SLOT, 1)
            for k, number in enumerate(Y_LISTS[side]):
                target = lanes - SLOT + k
                moved = pltpu.roll(values[number], target + side, 1)
                acc = jnp.where(lane == target, moved, acc)
            done.append(acc)
        return tuple(done)

    def send(step, source):
        def face(slots):
            for side in range(2):
                at = 0 if side == 0 else rows - 1
                for k in slots:
                    send_x[step, side, k] = source[X_LISTS[side][k], :, at, :]

        pairs = [
            (send_x.at[step, 0], recv_x.at[step, 0]),
            (send_x.at[step, 1], recv_x.at[step, 1]),
            (send_y.at[step, 0], recv_y.at[step, 0]),
            (send_y.at[step, 1], recv_y.at[step, 1]),
            (send_x.at[step, 0, 1], recv_c.at[step, 0]),
            (send_x.at[step, 1, 1], recv_c.at[step, 1]),
            (send_x.at[step, 0, 2], recv_c.at[step, 2]),
            (send_x.at[step, 1, 2], recv_c.at[step, 3]),
        ]
        copies = [
            pltpu.make_async_remote_copy(
                src_ref=source_ref,
                dst_ref=target_ref,
                send_sem=send_sem.at[step, number],
                recv_sem=recv_sem.at[step, number],
                device_id=device,
                device_id_type=MESH,
            )
            for number, ((source_ref, target_ref), device) in enumerate(zip(pairs, neighbours))
        ]
        face((1, 2))
        for copy in copies[4:] + copies[2:4]:
            copy.start()
        face((0, 3, 4, 5))
        for copy in copies[:2]:
            copy.start()
        return copies

    loads[0].wait()
    loads[1].wait()
    for load in loads[2:]:
        load.start()

    def first_pack(z, packed):
        values = {n: field[0, n, z] for side in Y_LISTS for n in side}
        return insert(packed, values)

    empty = (jnp.zeros((rows, lanes), jnp.float32),) * 2
    packed = lax.fori_loop(0, planes, first_pack, empty, unroll=8)
    send_y[0, 0] = packed[0]
    send_y[0, 1] = packed[1]
    pl.semaphore_wait(barrier, len(neighbours))
    started = [send(0, field.at[0])]
    def prepare_step(step, into):
        def prepare(z, carry):
            f = [sf[step, n, z].astype(jnp.float32) for n in range(flow)]
            h = [st[step, n, z].astype(jnp.float32) for n in range(COUNT - flow)]
            for k, value in enumerate(macros(f, h)):
                into[k, z] = value
            return carry

        lax.fori_loop(0, planes, prepare, 0, unroll=4)

    buffers = [field.at[step % 2] for step in range(steps - 1)] + [field_out]

    for step in range(steps):
        saved = steps - 1 - step
        source = buffers[step]

        def turn_plane(z, carry):
            for number in range(COUNT):
                cx, cy, _ = SPEEDS[number]
                if cx or cy:
                    source[number, z] = turn(source[number, z], cx, cy, rows, lanes)
            return carry

        lax.fori_loop(0, planes, turn_plane, 0, unroll=2)
        if step == 0:
            for load in loads[2:]:
                load.wait()
        prepare_step(saved, macro_out if saved == 0 else macro.at[saved])
        for copy in started[step]:
            copy.wait_recv()
        for corner, number in enumerate(CORNERS):
            side = 0 if SPEEDS[number][0] == 1 else 1
            end = ends[0] if SPEEDS[number][1] == 1 else ends[1]
            k = X_LISTS[side].index(number)
            merged = jnp.where(end, recv_c[step, corner], recv_x[step, side, k])
            recv_x[step, side, k] = turn(merged, 0, SPEEDS[number][1], rows, lanes)
        if step == steps - 1:
            halo_x_out[...] = recv_x[step]
            halo_y_out[...] = recv_y[step]
            break
        target = buffers[step + 1]
        halo_x = recv_x.at[step]

        def plane(z, carry):
            got, packed = carry
            pulled = pull_plane(z, source, halo_x, got, ends, edges)
            ux, uy, uz, cr = [macro[saved, k, z] for k in range(4)]
            f_out, h_out = transpose_collision(
                pulled[:flow], pulled[flow:], ux, uy, uz, cr, lab[z]
            )
            values = f_out + h_out
            for number in range(COUNT):
                target[number, z] = values[number]
            got = tuple(pltpu.roll(value, lanes - SLOT, 1) for value in got)
            return got, insert(packed, values)

        got = (recv_y[step, 0], recv_y[step, 1])
        got, packed = lax.fori_loop(0, planes, plane, (got, empty), unroll=8)
        send_y[step + 1, 0] = packed[0]
        send_y[step + 1, 1] = packed[1]
        started.append(send(step + 1, target))
    for copies in started:
        for copy in copies:
            copy.wait_send()


def finish(field, macro, halo_x, halo_y, lab, of_hbm, ot_hbm, stage, out_sem):
    planes, rows, lanes = field.shape[1:]
    flow = of_hbm.shape[0]
    _, ends, edges = tiles(rows, lanes)

    def stores(z):
        return [
            pltpu.make_async_copy(
                stage.at[pl.ds(0, flow), z], of_hbm.at[:, z], out_sem.at[0, z]
            ),
            pltpu.make_async_copy(
                stage.at[pl.ds(flow, COUNT - flow), z], ot_hbm.at[:, z], out_sem.at[1, z]
            ),
        ]

    got = (halo_y[0], halo_y[1])
    for z in range(planes):
        pulled = pull_plane(z, field, halo_x, got, ends, edges)
        ux, uy, uz, cr = [macro[k, z] for k in range(4)]
        f_out, h_out = transpose_collision(
            pulled[:flow], pulled[flow:], ux, uy, uz, cr, lab[z]
        )
        for number, value in enumerate(f_out + h_out):
            stage[number, z] = value
        for store in stores(z):
            store.start()
        got = tuple(pltpu.roll(value, lanes - SLOT, 1) for value in got)
    for z in range(planes):
        for store in stores(z):
            store.wait()


def body(saved_fluid, saved_tracer, adjoint_fluid, adjoint_tracer, label):
    steps, flow, planes, rows, lanes = saved_fluid.shape
    tracer = saved_tracer.shape[1]
    f32 = jnp.float32
    tile = (rows, lanes)
    whole = (flow + tracer, planes) + tile
    vmem, hbm = pl.BlockSpec(memory_space=pltpu.VMEM), pl.BlockSpec(memory_space=IN_SPACE)
    ready = pl.pallas_call(
        kernel,
        out_shape=(
            jax.ShapeDtypeStruct(whole, f32),
            jax.ShapeDtypeStruct((4, planes) + tile, f32),
            jax.ShapeDtypeStruct((2, 6, planes, lanes), f32),
            jax.ShapeDtypeStruct((2,) + tile, f32),
            jax.ShapeDtypeStruct(label.shape, label.dtype),
        ),
        in_specs=[hbm] * 5,
        out_specs=[vmem] * 5,
        scratch_shapes=[
            pltpu.VMEM(saved_fluid.shape, saved_fluid.dtype),
            pltpu.VMEM(saved_tracer.shape, saved_tracer.dtype),
            pltpu.VMEM((2,) + whole, f32),
            pltpu.VMEM((steps, 4, planes) + tile, f32),
            pltpu.VMEM((steps, 2, 6, planes, lanes), f32),
            pltpu.VMEM((steps, 2, 6, planes, lanes), f32),
            pltpu.VMEM((steps, 2) + tile, f32),
            pltpu.VMEM((steps, 2) + tile, f32),
            pltpu.VMEM((steps, 4, planes, lanes), f32),
            pltpu.SemaphoreType.DMA((5,)),
            pltpu.SemaphoreType.DMA((steps, 8)),
            pltpu.SemaphoreType.DMA((steps, 8)),
        ],
        compiler_params=pltpu.CompilerParams(
            collective_id=0, has_side_effects=True, vmem_limit_bytes=FIRST_VMEM
        ),
        name="adjoint_steps",
    )(*[pltpu.with_memory_space_constraint(value, pltpu.HBM) for value in (saved_fluid, saved_tracer, adjoint_fluid, adjoint_tracer, label)])
    return pl.pallas_call(
        finish,
        out_shape=(
            jax.ShapeDtypeStruct(adjoint_fluid.shape, f32),
            jax.ShapeDtypeStruct(adjoint_tracer.shape, f32),
        ),
        in_specs=[vmem] * 5,
        out_specs=[pl.BlockSpec(memory_space=pl.ANY)] * 2,
        scratch_shapes=[
            pltpu.VMEM(whole, f32),
            pltpu.SemaphoreType.DMA((2, planes)),
        ],
        compiler_params=pltpu.CompilerParams(vmem_limit_bytes=16 * 1024 * 1024),
        name="last_step",
    )(*ready)


def solution(mesh):
    placed = (
        P(None, None, None, "gx", "gy"),
        P(None, None, None, "gx", "gy"),
        P(None, None, "gx", "gy"),
        P(None, None, "gx", "gy"),
        P(None, "gx", "gy"),
    )
    return jax.shard_map(
        body,
        mesh=mesh,
        in_specs=placed,
        out_specs=(P(None, None, "gx", "gy"), P(None, None, "gx", "gy")),
        check_vma=False,
    )
```
